32 devices in a mesh: groups: 2 (over x), row: 16 (over z, y, core).
Axes of the slice: x: 2, y: 2, z: 4, core: 2. Of those that a mesh axis runs over, the one named last changes fastest.
Arguments:
- blocks: bfloat16 [128, 14, 128, 128], P(('groups', 'row')), parts along dimension 0, may hold values from -1.2 to 1.2
- block_cols: int32 [128, 14], P('groups'), parts along dimension 0, may hold values from 0 to 63, as said below
- kept_cols: int32 [128, 14], P('groups'), parts along dimension 0, may hold values from 0 to 63, as said below
Outputs:
- square: float32 [128, 14, 128, 128], P(('groups', 'row')), parts along dimension 0
- new_blocks: float32 [128, 14, 128, 128], P(('groups', 'row')), parts along dimension 0
The draws below stay inside these ranges and needn't reach their ends.
There are 2 independent parts, one for each index of `groups`. The reference program is written for one: setup_inputs(seed, part) draws one part's arguments, and reference() takes and returns one part's arrays. A program takes and returns all parts, laid end to end along the dimension named above; each array names one. Nothing has to cross between parts.
Inputs may be any that keep to these rules, and one draw needn't show every extreme that they name: `block_cols`: block row i is cell i % 4 of layer i // 4 of a periodic box of 16 layers. Slot 0 of row i holds i itself; the entries of a row are distinct cells whose layers lie within 2 of i's layer, cyclically. `kept_cols`: block row i is cell i % 4 of layer i // 4 of a periodic box of 16 layers. Slot 0 of row i holds i itself; the entries of a row are distinct cells whose layers lie within 2 of i's layer, cyclically.
All inputs are finite; a program needn't handle non-finite values.
Results may differ from the reference program's by a relative error of at most 0.0031.
Values may be sent and summed in bfloat16 or wider, within the bound.
A program may use at most 128 MiB of HBM per device.

```python
import jax
import jax.numpy as jnp
from jax import lax

B = 128
K = 14
KP = 14
REACH = 2
BR = 4
NB = 64


def draw_pattern(key, count):
    layer_count = NB // BR
    span = (2 * REACH + 1) * BR
    steps = jnp.arange(2 * REACH + 1, dtype=jnp.int32)
    layer_steps = jnp.where(steps % 2 == 1, -((steps + 1) // 2), steps // 2).astype(jnp.int32)
    slots = jnp.arange(span, dtype=jnp.int32)
    row_ids = jnp.arange(NB, dtype=jnp.int32)
    near_layer = jnp.mod(row_ids[:, None] // BR + layer_steps[slots // BR][None, :], layer_count)
    candidates = (near_layer * BR + (slots % BR)[None, :]).astype(jnp.int32)
    is_self = candidates == row_ids[:, None]
    row_keys = jax.random.split(key, NB)
    ranks = jax.vmap(lambda one_key: jax.random.permutation(one_key, span))(row_keys).astype(jnp.int32)
    ranks = jnp.where(row_ids[:, None] == 0, slots[None, :], ranks)
    scores = jnp.where(is_self, span, ranks).astype(jnp.int32)
    order = jnp.argsort(scores, axis=1, stable=True)
    chosen = jnp.take_along_axis(candidates, order[:, :count - 1], axis=1)
    return jnp.concatenate([row_ids[:, None], chosen], axis=1).astype(jnp.int32)


def draw_block_cols(key, part):
    key = jax.random.fold_in(key, 11)
    return draw_pattern(key, K)


def draw_kept_cols(key, part):
    key = jax.random.fold_in(key, 23)
    return draw_pattern(key, KP)


def draw_blocks(key, part):
    key = jax.random.fold_in(key, 37)
    noise_key, size_key, sign_key = jax.random.split(key, 3)
    array_shape = (NB, K, B, B)
    noise = jnp.clip(0.05 * jax.random.normal(noise_key, array_shape, jnp.float32), -0.2, 0.2)
    magnitude = jax.random.uniform(size_key, (NB, B), jnp.float32, 0.3, 0.9)
    signs = jnp.where(jax.random.bernoulli(sign_key, 0.5, (NB, B)), 1.0, -1.0)
    identity_block = jnp.eye(B, dtype=jnp.float32)
    slot_zero = (jnp.arange(K) == 0).astype(jnp.float32)
    diagonal = (signs * magnitude)[:, None, :, None] * identity_block * slot_zero[None, :, None, None]
    return (noise + diagonal).astype(jnp.bfloat16)


def setup_inputs(seed: int = 0, part: int = 0) -> dict:
    seeds = jax.random.split(jax.random.key(seed), 4)
    part_keys = jax.random.split(jax.random.fold_in(seeds[3], part), 4)
    return {
        "blocks": draw_blocks(jax.random.fold_in(jax.random.fold_in(seeds[3], part), 71), part),
        "block_cols": draw_block_cols(jax.random.fold_in(jax.random.fold_in(seeds[3], part), 71), part),
        "kept_cols": draw_kept_cols(jax.random.fold_in(jax.random.fold_in(seeds[3], part), 71), part),
    }


def pick_blocks(flattened, slot_count, row_pattern, needed, positions, wanted):
    pattern_rows = row_pattern[needed]
    matches = pattern_rows[:, :, None] == wanted[None, None, :]
    columns = jnp.arange(slot_count, dtype=jnp.int32)
    located = jnp.sum(jnp.where(matches, columns[None, :, None], 0), axis=1).astype(jnp.int32)
    present = jnp.any(matches, axis=1)
    picked = flattened[positions.astype(jnp.int32)[:, None] * slot_count + located]
    return jnp.where(present[:, :, None, None], picked, jnp.zeros_like(picked))


def reference(blocks, block_cols, kept_cols):
    flat_blocks = blocks.reshape(-1, B, B)

    def square_row(packed):
        own_row, needed, wanted = packed
        picked = pick_blocks(flat_blocks, K, block_cols, needed, needed, wanted)
        return jnp.einsum('kxy,kpyz->pxz', own_row.astype(jnp.float32), picked.astype(jnp.float32))

    square = lax.map(square_row, (blocks, block_cols, kept_cols))
    row_ids = jnp.arange(NB, dtype=jnp.int32)
    diagonal_mask = (kept_cols == row_ids[:, None]).astype(jnp.float32)
    identity_block = jnp.eye(B, dtype=jnp.float32)
    factor = (3.0 * diagonal_mask[:, :, None, None] * identity_block - square).astype(jnp.bfloat16)
    flat_factor = factor.reshape(-1, B, B)

    def new_row(packed):
        own_row, needed = packed
        picked = pick_blocks(flat_factor, KP, kept_cols, needed, needed, needed)
        return 0.5 * jnp.einsum('kxy,kqyz->qxz', own_row.astype(jnp.float32), picked.astype(jnp.float32))

    new_blocks = lax.map(new_row, (blocks, block_cols))
    return (square, new_blocks)
```

```python
import functools

import jax
import jax.numpy as jnp
from jax import lax
from jax.experimental import pallas as pl
from jax.experimental.pallas import tpu as pltpu
from jax.sharding import PartitionSpec as P

MESH = pl.DeviceIdType.MESH
LAYERS = 5
HALVES = 2


def window_layers(me, count):
    core, side = me % 2, (me // 2) % 2
    away = jnp.where(side == 0, 1, -1)
    return [
        me,
        me + 1 - 2 * core,
        (me + 2 * away + count) % count,
        (me - 2 * away + count) % count,
        (me - 1 + 2 * core + count) % count,
    ]


def tables(block_cols, kept_cols, me, count, rows):
    layers = jnp.stack(window_layers(me, count)).astype(jnp.int32)
    ids = (layers[:, None] * rows + jnp.arange(rows, dtype=jnp.int32)).reshape(-1)

    def slots(cols):
        near = cols[ids]
        match = near[:, :, None] == ids[None, None, :]
        slot = jnp.arange(cols.shape[1], dtype=jnp.int32)[None, :, None]
        return jnp.max(jnp.where(match, slot, -1), axis=1)

    def places(cols):
        own = lax.dynamic_slice_in_dim(cols, me * rows, rows, 0)
        match = own[:, :, None] == ids[None, None, :]
        place = jnp.arange(ids.shape[0], dtype=jnp.int32)
        return jnp.sum(jnp.where(match, place, 0), axis=2)

    parts = [slots(block_cols), slots(kept_cols), places(kept_cols), places(block_cols)]
    return jnp.concatenate([part.reshape(-1) for part in parts]).astype(jnp.int32)


def kernel(count, rows, slots, kept, x_ref, tab, sq_out, new_out, own_f, a, d, sq, new,
           send_sem, recv_sem, out_sem, *bufs):
    width = x_ref.shape[-1]
    span = LAYERS * rows
    pairs = rows // 2
    me = lax.axis_index("row")
    core, side = me % 2, (me // 2) % 2
    mate = me + 1 - 2 * core
    across = me + 2 - 4 * side
    onward = (me + 4 - 8 * side + count) % count
    behind = (me - 4 + 8 * side + count) % count
    shares_first = core == side

    barrier = pltpu.get_barrier_semaphore()
    for other in (mate, across, onward, behind):
        pl.semaphore_signal(barrier, inc=1, device_id={"row": other}, device_id_type=MESH)
    pl.semaphore_wait(barrier, 4)

    slots_at = (0, span * span)
    kept_at = 2 * span * span
    cols_at = kept_at + rows * kept
    depth = (slots, kept)
    pieces = rows * HALVES

    def landing(stage, source, piece):
        row, half = piece // HALVES, piece % HALVES
        length = depth[stage] // HALVES
        ref = bufs[(stage * 4 + source) * pairs + row // 2]
        return ref.at[row % 2, pl.ds(half * length, length)]

    def copy(stage, source, piece, src, device):
        return pltpu.make_async_remote_copy(
            src_ref=src,
            dst_ref=landing(stage, source, piece),
            send_sem=send_sem.at[stage, source, piece],
            recv_sem=recv_sem.at[stage, source, piece],
            device_id={"row": device},
            device_id_type=MESH,
        )

    def own_piece(stage, piece):
        row, half = piece // HALVES, piece % HALVES
        length = depth[stage] // HALVES
        ref = (x_ref, own_f)[stage]
        return ref.at[row, pl.ds(half * length, length)]

    def to_mate(stage, piece):
        return copy(stage, 0, piece, own_piece(stage, piece), mate)

    def to_across(stage, piece):
        return copy(stage, 1, piece, own_piece(stage, piece), across)

    def to_onward(stage, piece):
        return copy(stage, 2, piece, landing(stage, 1, piece), onward)

    def share(stage, piece, source):
        return copy(stage, 3, piece, landing(stage, source, piece), mate)

    def start_own(stage, row):
        for half in range(HALVES):
            to_across(stage, row * HALVES + half).start()
        for half in range(HALVES):
            to_mate(stage, row * HALVES + half).start()

    def block(ref, row, slot):
        value = ref[row, jnp.maximum(slot, 0)]
        return jnp.where(slot >= 0, value, jnp.zeros_like(value))

    def multiply(stage, source, pair):
        first = source == 0 and pair == 0
        if source == 0:
            ref, base = (x_ref, own_f)[stage], 2 * pair
        else:
            ref, base = bufs[(stage * 4 + source - 1) * pairs + pair], 0
        line = slots_at[stage] + (source * rows + 2 * pair) * span

        def body(step, carry):
            lines = []
            for row in range(2):
                at = line + row * span + 2 * step
                lines.append(jnp.concatenate(
                    [block(ref, base + row, tab[at]), block(ref, base + row, tab[at + 1])], axis=1))
            right = jnp.concatenate(lines, axis=0)
            part = jnp.dot(a[source * pairs + pair], right, preferred_element_type=jnp.float32)
            for col in range(2):
                piece = part[:, col * width:(col + 1) * width]
                if first:
                    d[2 * step + col] = piece
                else:
                    d[2 * step + col] += piece
            return carry

        lax.fori_loop(0, span // 2, body, 0)

    def gather_and_multiply(stage):
        for pair in range(pairs):
            multiply(stage, 0, pair)
        for piece in range(pieces):
            to_mate(stage, piece).wait_recv()
        for pair in range(pairs):
            multiply(stage, 1, pair)
        per_pair = 2 * HALVES
        lag = 2
        for step in range(pieces + lag):
            if step < pieces:
                to_across(stage, step).wait_recv()
                to_onward(stage, step).start()

                @pl.when(shares_first)
                def _():
                    share(stage, step, 1).start()

            late = step - lag
            if late >= 0:
                to_onward(stage, late).wait_recv()

                @pl.when(jnp.logical_not(shares_first))
                def _():
                    share(stage, late, 2).start()

            if step < pieces and (step + 1) % per_pair == 0:
                multiply(stage, 2, step // per_pair)
            if late >= 0 and (late + 1) % per_pair == 0:
                pair = late // per_pair
                multiply(stage, 3, pair)
                for piece in range(pair * per_pair, (pair + 1) * per_pair):
                    share(stage, piece, 1).wait_recv()
                multiply(stage, 4, pair)

    for row in range(rows):
        start_own(0, row)

    def build(step, carry):
        for row in range(rows):
            for col in range(2):
                slot = tab[row * span + 2 * step + col]
                a[step, row * width:(row + 1) * width, col * width:(col + 1) * width] = block(
                    x_ref, row, slot)
        return carry

    lax.fori_loop(0, LAYERS * pairs, build, 0)
    gather_and_multiply(0)

    eye = (lax.broadcasted_iota(jnp.int32, (width, width), 0)
           == lax.broadcasted_iota(jnp.int32, (width, width), 1)).astype(jnp.float32)
    for row in range(rows):
        def pick(slot, carry):
            place = tab[kept_at + row * kept + slot]
            value = d[place, row * width:(row + 1) * width, :]
            sq[row, slot] = value
            three = jnp.where(place == row, 3.0, 0.0)
            own_f[row, slot] = (three * eye - value).astype(jnp.bfloat16)
            return carry

        lax.fori_loop(0, kept, pick, 0)
        start_own(1, row)
        pltpu.make_async_copy(sq.at[row], sq_out.at[row], out_sem.at[0, row]).start()

    gather_and_multiply(1)

    for row in range(rows):
        def pick(slot, carry):
            place = tab[cols_at + row * slots + slot]
            new[row, slot] = 0.5 * d[place, row * width:(row + 1) * width, :]
            return carry

        lax.fori_loop(0, slots, pick, 0)
        pltpu.make_async_copy(new.at[row], new_out.at[row], out_sem.at[1, row]).start()

    for stage in range(2):
        for piece in range(pieces):
            to_mate(stage, piece).wait_send()
            to_across(stage, piece).wait_send()
            to_onward(stage, piece).wait_send()
            share(stage, piece, 1).wait_send()
    for row in range(rows):
        pltpu.make_async_copy(sq.at[row], sq_out.at[row], out_sem.at[0, row]).wait()
        pltpu.make_async_copy(new.at[row], new_out.at[row], out_sem.at[1, row]).wait()


def local(count, blocks, block_cols, kept_cols):
    rows, slots, width, _ = blocks.shape
    kept = kept_cols.shape[1]
    me = lax.axis_index("row")
    table = tables(block_cols, kept_cols, me, count, rows)
    span = LAYERS * rows
    pieces = rows * HALVES
    landings = [
        pltpu.VMEM((2, depth, width, width), jnp.bfloat16)
        for depth in (slots, kept)
        for _ in range(4 * (rows // 2))
    ]
    return pl.pallas_call(
        functools.partial(kernel, count, rows, slots, kept),
        out_shape=(
            jax.ShapeDtypeStruct((rows, kept, width, width), jnp.float32),
            jax.ShapeDtypeStruct((rows, slots, width, width), jnp.float32),
        ),
        in_specs=[pl.BlockSpec(memory_space=pltpu.VMEM), pl.BlockSpec(memory_space=pltpu.SMEM)],
        out_specs=(pl.BlockSpec(memory_space=pl.ANY), pl.BlockSpec(memory_space=pl.ANY)),
        scratch_shapes=[
            pltpu.VMEM((rows, kept, width, width), jnp.bfloat16),
            pltpu.VMEM((LAYERS * rows // 2, rows * width, 2 * width), jnp.bfloat16),
            pltpu.VMEM((span, rows * width, width), jnp.float32),
            pltpu.VMEM((rows, kept, width, width), jnp.float32),
            pltpu.VMEM((rows, slots, width, width), jnp.float32),
            pltpu.SemaphoreType.DMA((2, 4, pieces)),
            pltpu.SemaphoreType.DMA((2, 4, pieces)),
            pltpu.SemaphoreType.DMA((2, rows)),
        ] + landings,
        compiler_params=pltpu.CompilerParams(
            collective_id=0, has_side_effects=True, vmem_limit_bytes=48 * 1024 * 1024
        ),
    )(blocks, table)


def solution(mesh):
    count = mesh.shape["row"]
    in_specs = (P(("groups", "row"), None, None, None), P("groups", None), P("groups", None))
    out_specs = (P(("groups", "row"), None, None, None), P(("groups", "row"), None, None, None))
    return jax.shard_map(
        functools.partial(local, count), mesh=mesh, in_specs=in_specs, out_specs=out_specs,
        check_vma=False)
```

```python
import functools

import jax
import jax.numpy as jnp
from jax import lax
from jax.experimental import pallas as pl
from jax.experimental.pallas import tpu as pltpu
from jax.sharding import PartitionSpec as P

MESH = pl.DeviceIdType.MESH
LAYERS = 5
HALVES = 2


def window_layers(me, count):
    core, side = me % 2, (me // 2) % 2
    away = jnp.where(side == 0, 1, -1)
    return [
        me,
        me + 1 - 2 * core,
        (me + 2 * away + count) % count,
        (me - 2 * away + count) % count,
        (me - 1 + 2 * core + count) % count,
    ]


def table_rows(span, slots, kept):
    starts = [0]
    for length in (span, span, kept, slots):
        starts.append(starts[-1] + (length + 7) // 8 * 8)
    return starts


def fill_tables(cols_ref, kept_ref, out, layers, rows, starts):
    span = LAYERS * rows
    line = lax.broadcasted_iota(jnp.int32, (span, cols_ref.shape[1]), 0)
    ids = jnp.zeros_like(line)
    for index, layer in enumerate(layers):
        ids = jnp.where(line // rows == index, layer * rows + line % rows, ids)
    for start, ref in zip(starts[:2], (cols_ref, kept_ref)):
        found = jnp.full_like(ids, -1)
        for slot in range(ref.shape[0]):
            found = jnp.where(ref[slot:slot + 1, :] == ids, slot, found)
        out[start:start + span, :] = found
    for start, ref in zip(starts[2:4], (kept_ref, cols_ref)):
        cols = ref[...]
        place = jnp.zeros_like(cols)
        for index, layer in enumerate(layers):
            for row in range(rows):
                place = jnp.where(cols == layer * rows + row, index * rows + row, place)
        out[start:start + ref.shape[0], :] = place


def kernel(count, rows, slots, kept, x_hbm, cols_ref, kept_ref, sq_out, new_out, x_ref, tab, found,
           own_f, a, d, sq, new, send_sem, recv_sem, out_sem, in_sem, *bufs):
    width = x_ref.shape[-1]
    load_x = pltpu.make_async_copy(x_hbm, x_ref, in_sem.at[0])
    load_x.start()
    span = LAYERS * rows
    pairs = rows // 2
    me = lax.axis_index("row")
    core, side = me % 2, (me // 2) % 2
    mate = me + 1 - 2 * core
    across = me + 2 - 4 * side
    onward = (me + 4 - 8 * side + count) % count
    behind = (me - 4 + 8 * side + count) % count
    shares_first = core == side

    barrier = pltpu.get_barrier_semaphore()
    for other in (mate, across, onward, behind):
        pl.semaphore_signal(barrier, inc=1, device_id={"row": other}, device_id_type=MESH)
    pl.semaphore_wait(barrier, 4)

    starts = table_rows(span, slots, kept)
    layers = window_layers(me, count)
    depth = (slots, kept)
    pieces = rows * HALVES

    def landing(stage, source, piece):
        row, half = piece // HALVES, piece % HALVES
        length = depth[stage] // HALVES
        ref = bufs[(stage * 4 + source) * pairs + row // 2]
        return ref.at[row % 2, pl.ds(half * length, length)]

    def copy(stage, source, piece, src, device):
        return pltpu.make_async_remote_copy(
            src_ref=src,
            dst_ref=landing(stage, source, piece),
            send_sem=send_sem.at[stage, source, piece],
            recv_sem=recv_sem.at[stage, source, piece],
            device_id={"row": device},
            device_id_type=MESH,
        )

    def own_piece(stage, piece):
        row, half = piece // HALVES, piece % HALVES
        length = depth[stage] // HALVES
        ref = (x_hbm, own_f)[stage]
        return ref.at[row, pl.ds(half * length, length)]

    def to_mate(stage, piece):
        return copy(stage, 0, piece, own_piece(stage, piece), mate)

    def to_across(stage, piece):
        return copy(stage, 1, piece, own_piece(stage, piece), across)

    def to_onward(stage, piece):
        return copy(stage, 2, piece, landing(stage, 1, piece), onward)

    def share(stage, piece, source):
        return copy(stage, 3, piece, landing(stage, source, piece), mate)

    def start_own(stage, row):
        for half in range(HALVES):
            to_across(stage, row * HALVES + half).start()
        for half in range(HALVES):
            to_mate(stage, row * HALVES + half).start()

    def block(ref, row, slot):
        value = ref[row, jnp.maximum(slot, 0)]
        return jnp.where(slot >= 0, value, jnp.zeros_like(value))

    def multiply(stage, source, pair):
        first = source == 0 and pair == 0
        if source == 0:
            ref, base = (x_ref, own_f)[stage], 2 * pair
        else:
            ref, base = bufs[(stage * 4 + source - 1) * pairs + pair], 0
        line = layers[source] * rows + 2 * pair

        def body(step, carry):
            lines = []
            for row in range(2):
                lines.append(jnp.concatenate(
                    [block(ref, base + row, tab[starts[stage] + 2 * step + col, line + row]) for col in range(2)], axis=1))
            right = jnp.concatenate(lines, axis=0)
            part = jnp.dot(a[source * pairs + pair], right, preferred_element_type=jnp.float32)
            for col in range(2):
                piece = part[:, col * width:(col + 1) * width]
                if first:
                    d[2 * step + col] = piece
                else:
                    d[2 * step + col] += piece
            return carry

        lax.fori_loop(0, span // 2, body, 0, unroll=10)

    def gather_and_multiply(stage):
        for pair in range(pairs):
            multiply(stage, 0, pair)
        for piece in range(pieces):
            to_mate(stage, piece).wait_recv()
        for pair in range(pairs):
            multiply(stage, 1, pair)
        per_pair = 2 * HALVES
        lag = 2
        for step in range(pieces + lag):
            if step < pieces:
                to_across(stage, step).wait_recv()
                to_onward(stage, step).start()

                @pl.when(shares_first)
                def _():
                    share(stage, step, 1).start()

            late = step - lag
            if late >= 0:
                to_onward(stage, late).wait_recv()

                @pl.when(jnp.logical_not(shares_first))
                def _():
                    share(stage, late, 2).start()

            if step < pieces and (step + 1) % per_pair == 0:
                multiply(stage, 2, step // per_pair)
            if late >= 0 and (late + 1) % per_pair == 0:
                pair = late // per_pair
                multiply(stage, 3, pair)
                for piece in range(pair * per_pair, (pair + 1) * per_pair):
                    share(stage, piece, 1).wait_recv()
                multiply(stage, 4, pair)

    for row in range(rows):
        start_own(0, row)
    fill_tables(cols_ref, kept_ref, found, layers, rows, starts)
    load_tab = pltpu.make_async_copy(found, tab, in_sem.at[1])
    load_tab.start()
    load_tab.wait()
    load_x.wait()

    def build(step, carry):
        for row in range(rows):
            for col in range(2):
                slot = tab[2 * step + col, me * rows + row]
                a[step, row * width:(row + 1) * width, col * width:(col + 1) * width] = block(
                    x_ref, row, slot)
        return carry

    lax.fori_loop(0, LAYERS * pairs, build, 0)
    gather_and_multiply(0)

    eye = (lax.broadcasted_iota(jnp.int32, (width, width), 0)
           == lax.broadcasted_iota(jnp.int32, (width, width), 1)).astype(jnp.float32)
    for row in range(rows):
        def pick(slot, carry):
            place = tab[starts[2] + slot, me * rows + row]
            value = d[place, row * width:(row + 1) * width, :]
            sq[row, slot] = value
            three = jnp.where(place == row, 3.0, 0.0)
            own_f[row, slot] = (three * eye - value).astype(jnp.bfloat16)
            return carry

        lax.fori_loop(0, kept, pick, 0)
        start_own(1, row)
        pltpu.make_async_copy(sq.at[row], sq_out.at[row], out_sem.at[0, row]).start()

    gather_and_multiply(1)

    for row in range(rows):
        def pick(slot, carry):
            place = tab[starts[3] + slot, me * rows + row]
            new[row, slot] = 0.5 * d[place, row * width:(row + 1) * width, :]
            return carry

        lax.fori_loop(0, slots, pick, 0)
        pltpu.make_async_copy(new.at[row], new_out.at[row], out_sem.at[1, row]).start()

    for stage in range(2):
        for piece in range(pieces):
            to_mate(stage, piece).wait_send()
            to_across(stage, piece).wait_send()
            to_onward(stage, piece).wait_send()
            share(stage, piece, 1).wait_send()
    for row in range(rows):
        pltpu.make_async_copy(sq.at[row], sq_out.at[row], out_sem.at[0, row]).wait()
        pltpu.make_async_copy(new.at[row], new_out.at[row], out_sem.at[1, row]).wait()


def local(count, blocks, block_cols, kept_cols):
    rows, slots, width, _ = blocks.shape
    kept = kept_cols.shape[1]
    span = LAYERS * rows
    pieces = rows * HALVES
    landings = [
        pltpu.VMEM((2, depth, width, width), jnp.bfloat16)
        for depth in (slots, kept)
        for _ in range(4 * (rows // 2))
    ]
    return pl.pallas_call(
        functools.partial(kernel, count, rows, slots, kept),
        out_shape=(
            jax.ShapeDtypeStruct((rows, kept, width, width), jnp.float32),
            jax.ShapeDtypeStruct((rows, slots, width, width), jnp.float32),
        ),
        in_specs=[pl.BlockSpec(memory_space=pl.ANY)] + [pl.BlockSpec(memory_space=pltpu.VMEM)] * 2,
        out_specs=(pl.BlockSpec(memory_space=pl.ANY), pl.BlockSpec(memory_space=pl.ANY)),
        scratch_shapes=[
            pltpu.VMEM((rows, slots, width, width), jnp.bfloat16),
            pltpu.SMEM((table_rows(span, slots, kept)[-1], block_cols.shape[0]), jnp.int32),
            pltpu.VMEM((table_rows(span, slots, kept)[-1], block_cols.shape[0]), jnp.int32),
            pltpu.VMEM((rows, kept, width, width), jnp.bfloat16),
            pltpu.VMEM((LAYERS * rows // 2, rows * width, 2 * width), jnp.bfloat16),
            pltpu.VMEM((span, rows * width, width), jnp.float32),
            pltpu.VMEM((rows, kept, width, width), jnp.float32),
            pltpu.VMEM((rows, slots, width, width), jnp.float32),
            pltpu.SemaphoreType.DMA((2, 4, pieces)),
            pltpu.SemaphoreType.DMA((2, 4, pieces)),
            pltpu.SemaphoreType.DMA((2, rows)),
            pltpu.SemaphoreType.DMA((2,)),
        ] + landings,
        compiler_params=pltpu.CompilerParams(
            collective_id=0, has_side_effects=True, vmem_limit_bytes=60 * 1024 * 1024
        ),
    )(blocks, block_cols.T, kept_cols.T)


def solution(mesh):
    count = mesh.shape["row"]
    in_specs = (P(("groups", "row"), None, None, None), P("groups", None), P("groups", None))
    out_specs = (P(("groups", "row"), None, None, None), P(("groups", "row"), None, None, None))
    return jax.shard_map(
        functools.partial(local, count), mesh=mesh, in_specs=in_specs, out_specs=out_specs,
        check_vma=False)
```

```python
import functools

import jax
import jax.numpy as jnp
from jax import lax
from jax.experimental import pallas as pl
from jax.experimental.pallas import tpu as pltpu
from jax.sharding import PartitionSpec as P

MESH = pl.DeviceIdType.MESH
LAYERS = 5
HALVES = 2


def window_layers(me, count):
    core, side = me % 2, (me // 2) % 2
    away = jnp.where(side == 0, 1, -1)
    return [
        me,
        me + 1 - 2 * core,
        (me + 2 * away + count) % count,
        (me - 2 * away + count) % count,
        (me - 1 + 2 * core + count) % count,
    ]


def table_rows(span, slots, kept):
    starts = [0]
    for length in (span, span, kept, slots):
        starts.append(starts[-1] + (length + 7) // 8 * 8)
    return starts


def fill_tables(cols_ref, kept_ref, out, layers, rows, starts):
    span = LAYERS * rows
    line = lax.broadcasted_iota(jnp.int32, (span, cols_ref.shape[1]), 0)
    ids = jnp.zeros_like(line)
    for index, layer in enumerate(layers):
        ids = jnp.where(line // rows == index, layer * rows + line % rows, ids)
    for start, ref in zip(starts[:2], (cols_ref, kept_ref)):
        found = jnp.full_like(ids, -1)
        for slot in range(ref.shape[0]):
            found = jnp.where(ref[slot:slot + 1, :] == ids, slot, found)
        out[start:start + span, :] = found
    for start, ref in zip(starts[2:4], (kept_ref, cols_ref)):
        cols = ref[...]
        place = jnp.zeros_like(cols)
        for index, layer in enumerate(layers):
            for row in range(rows):
                place = jnp.where(cols == layer * rows + row, index * rows + row, place)
        out[start:start + ref.shape[0], :] = place


def kernel(count, rows, slots, kept, x_hbm, cols_ref, kept_ref, sq_out, new_out, x_ref, tab, found,
           a, d, sq, new, send_sem, recv_sem, out_sem, in_sem, *bufs):
    width = x_ref.shape[-1]
    part_width = width // HALVES
    load_x = pltpu.make_async_copy(x_hbm, x_ref, in_sem.at[0])
    load_x.start()
    span = LAYERS * rows
    pairs = rows // 2
    me = lax.axis_index("row")
    core, side = me % 2, (me // 2) % 2
    mate = me + 1 - 2 * core
    across = me + 2 - 4 * side
    onward = (me + 4 - 8 * side + count) % count
    behind = (me - 4 + 8 * side + count) % count
    shares_first = core == side
    own, bufs = bufs[:2 * HALVES], bufs[2 * HALVES:]

    barrier = pltpu.get_barrier_semaphore()
    for other in (mate, across, onward, behind):
        pl.semaphore_signal(barrier, inc=1, device_id={"row": other}, device_id_type=MESH)
    pl.semaphore_wait(barrier, 4)

    starts = table_rows(span, slots, kept)
    layers = window_layers(me, count)
    pieces = rows * HALVES

    def landed(source, piece):
        return bufs[(piece // 2) * 4 + source]

    def landing(source, piece):
        return landed(source, piece).at[piece % 2]

    def copy(source, piece, src, device):
        return pltpu.make_async_remote_copy(
            src_ref=src,
            dst_ref=landing(source, piece),
            send_sem=send_sem.at[source, piece],
            recv_sem=recv_sem.at[source, piece],
            device_id={"row": device},
            device_id_type=MESH,
        )

    def own_piece(piece):
        return own[piece // rows].at[piece % rows]

    def to_mate(piece):
        return copy(0, piece, own_piece(piece), mate)

    def to_across(piece):
        return copy(1, piece, own_piece(piece), across)

    def to_onward(piece):
        return copy(2, piece, landing(1, piece), onward)

    def share(piece, source):
        return copy(3, piece, landing(source, piece), mate)

    def block(ref, row, slot):
        value = ref[row, jnp.maximum(slot, 0)]
        return jnp.where(slot >= 0, value, jnp.zeros_like(value))

    def multiply(phase, source, pair):
        stage, half = phase // HALVES, phase % HALVES
        first = source == 0 and pair == 0
        if source == 0:
            ref, base = own[phase], 2 * pair
        else:
            ref, base = bufs[(phase * pairs + pair) * 4 + source - 1], 0
        line = layers[source] * rows + 2 * pair
        group = span // 2

        def body(step, carry):
            left = jnp.concatenate([
                jnp.concatenate(
                    [block(ref, base + row, tab[starts[stage] + group * step + col, line + row])
                     for row in range(2)], axis=1)
                for col in range(group)], axis=0)
            part = jnp.dot(left, a[source * pairs + pair], preferred_element_type=jnp.float32)
            for col in range(group):
                piece = part[col * part_width:(col + 1) * part_width]
                if first:
                    d[half, group * step + col] = piece
                else:
                    d[half, group * step + col] += piece
            return carry

        lax.fori_loop(0, 2, body, 0)

    def near(phase):
        for pair in range(pairs):
            multiply(phase, 0, pair)
        for piece in range(phase * rows, (phase + 1) * rows):
            to_mate(piece).wait_recv()
        for pair in range(pairs):
            multiply(phase, 1, pair)

    def finish(phase):
        stage, half = phase // HALVES, phase % HALVES
        for row in range(rows):
            lanes = pl.ds(row * width, width)
            columns = pl.ds(half * part_width, part_width)
            if stage == 0:
                line = lax.broadcasted_iota(jnp.int32, (part_width, width), 0) + half * part_width
                eye = (line == lax.broadcasted_iota(jnp.int32, (part_width, width), 1)).astype(
                    jnp.float32)

                def pick(slot, carry):
                    place = tab[starts[2] + slot, me * rows + row]
                    value = d[half, place, :, lanes]
                    sq[row, slot, :, columns] = value.T
                    three = jnp.where(place == row, 3.0, 0.0)
                    own[HALVES + half][row, slot] = (three * eye - value).astype(jnp.bfloat16)
                    return carry

                lax.fori_loop(0, kept, pick, 0)
                piece = pieces + half * rows + row
                to_across(piece).start()
                to_mate(piece).start()
                if half == HALVES - 1:
                    pltpu.make_async_copy(sq.at[row], sq_out.at[row], out_sem.at[0, row]).start()
            else:
                def pick(slot, carry):
                    place = tab[starts[3] + slot, me * rows + row]
                    new[row, slot, :, columns] = 0.5 * d[half, place, :, lanes].T
                    return carry

                lax.fori_loop(0, slots, pick, 0)
                if half == HALVES - 1:
                    pltpu.make_async_copy(new.at[row], new_out.at[row], out_sem.at[1, row]).start()

    load_x.wait()
    for half in range(HALVES):
        for row in range(rows):
            def turn(slot, carry):
                own[half][row, slot] = x_ref[row, slot].T[half * part_width:(half + 1) * part_width]
                return carry

            lax.fori_loop(0, slots, turn, 0)
            to_across(half * rows + row).start()
            to_mate(half * rows + row).start()

    fill_tables(cols_ref, kept_ref, found, layers, rows, starts)
    load_tab = pltpu.make_async_copy(found, tab, in_sem.at[1])
    load_tab.start()
    load_tab.wait()

    def build(step, carry):
        for row in range(rows):
            for col in range(2):
                slot = tab[2 * step + col, layers[0] * rows + row]
                for half in range(HALVES):
                    at = col * width + half * part_width
                    a[step, at:at + part_width, row * width:(row + 1) * width] = block(
                        own[half], row, slot)
        return carry

    lax.fori_loop(0, LAYERS * pairs, build, 0)
    near(0)
    near(1)

    lag = 2
    total = 2 * pieces
    for step in range(total + lag):
        if step < total:
            to_across(step).wait_recv()
            to_onward(step).start()

            @pl.when(shares_first)
            def _():
                share(step, 1).start()

        late = step - lag
        if late >= 0:
            to_onward(late).wait_recv()

            @pl.when(jnp.logical_not(shares_first))
            def _():
                share(late, 2).start()

        if step < total and step % 2 == 1:
            multiply(step // rows, 2, step % rows // 2)
        if late >= 0 and late % 2 == 1:
            phase, pair = late // rows, late % rows // 2
            multiply(phase, 3, pair)
            for piece in (late - 1, late):
                share(piece, 1).wait_recv()
            multiply(phase, 4, pair)
            if pair == pairs - 1:
                finish(phase)
                if phase + HALVES < 2 * HALVES:
                    near(phase + HALVES)

    for piece in range(total):
        to_mate(piece).wait_send()
        to_across(piece).wait_send()
        to_onward(piece).wait_send()
        share(piece, 1).wait_send()
    for row in range(rows):
        pltpu.make_async_copy(sq.at[row], sq_out.at[row], out_sem.at[0, row]).wait()
        pltpu.make_async_copy(new.at[row], new_out.at[row], out_sem.at[1, row]).wait()


def local(count, blocks, block_cols, kept_cols):
    rows, slots, width, _ = blocks.shape
    kept = kept_cols.shape[1]
    span = LAYERS * rows
    pieces = rows * HALVES
    half_width = width // HALVES
    own = [
        pltpu.VMEM((rows, depth, half_width, width), jnp.bfloat16)
        for depth in (slots, kept)
        for _ in range(HALVES)
    ]
    landings = [
        pltpu.VMEM((2, depth, half_width, width), jnp.bfloat16)
        for depth in (slots, kept)
        for _ in range(HALVES * 4 * (rows // 2))
    ]
    return pl.pallas_call(
        functools.partial(kernel, count, rows, slots, kept),
        out_shape=(
            jax.ShapeDtypeStruct((rows, kept, width, width), jnp.float32),
            jax.ShapeDtypeStruct((rows, slots, width, width), jnp.float32),
        ),
        in_specs=[pl.BlockSpec(memory_space=pl.ANY)] + [pl.BlockSpec(memory_space=pltpu.VMEM)] * 2,
        out_specs=(pl.BlockSpec(memory_space=pl.ANY), pl.BlockSpec(memory_space=pl.ANY)),
        scratch_shapes=[
            pltpu.VMEM((rows, slots, width, width), jnp.bfloat16),
            pltpu.SMEM((table_rows(span, slots, kept)[-1], block_cols.shape[0]), jnp.int32),
            pltpu.VMEM((table_rows(span, slots, kept)[-1], block_cols.shape[0]), jnp.int32),
            pltpu.VMEM((LAYERS * rows // 2, 2 * width, rows * width), jnp.bfloat16),
            pltpu.VMEM((HALVES, span, half_width, rows * width), jnp.float32),
            pltpu.VMEM((rows, kept, width, width), jnp.float32),
            pltpu.VMEM((rows, slots, width, width), jnp.float32),
            pltpu.SemaphoreType.DMA((4, 2 * pieces)),
            pltpu.SemaphoreType.DMA((4, 2 * pieces)),
            pltpu.SemaphoreType.DMA((2, rows)),
            pltpu.SemaphoreType.DMA((2,)),
        ] + own + landings,
        compiler_params=pltpu.CompilerParams(
            collective_id=0, has_side_effects=True, vmem_limit_bytes=60 * 1024 * 1024
        ),
    )(blocks, block_cols.T, kept_cols.T)


def solution(mesh):
    count = mesh.shape["row"]
    in_specs = (P(("groups", "row"), None, None, None), P("groups", None), P("groups", None))
    out_specs = (P(("groups", "row"), None, None, None), P(("groups", "row"), None, None, None))
    return jax.shard_map(
        functools.partial(local, count), mesh=mesh, in_specs=in_specs, out_specs=out_specs,
        check_vma=False)
```

```python
import functools

import jax
import jax.numpy as jnp
from jax import lax
from jax.experimental import pallas as pl
from jax.experimental.pallas import tpu as pltpu
from jax.sharding import PartitionSpec as P

MESH = pl.DeviceIdType.MESH
LAYERS = 5
HALVES = 2


def window_layers(me, count):
    core, side = me % 2, (me // 2) % 2
    away = jnp.where(side == 0, 1, -1)
    return [
        me,
        me + 1 - 2 * core,
        (me + 2 * away + count) % count,
        (me - 2 * away + count) % count,
        (me - 1 + 2 * core + count) % count,
    ]


def table_rows(span, slots, kept):
    starts = [0]
    for length in (span, span, kept, slots):
        starts.append(starts[-1] + (length + 7) // 8 * 8)
    return starts


def fill_tables(cols_ref, kept_ref, out, layers, rows, starts):
    span = LAYERS * rows
    line = lax.broadcasted_iota(jnp.int32, (span, cols_ref.shape[1]), 0)
    ids = jnp.zeros_like(line)
    for index, layer in enumerate(layers):
        ids = jnp.where(line // rows == index, layer * rows + line % rows, ids)
    for start, ref in zip(starts[:2], (cols_ref, kept_ref)):
        found = jnp.full_like(ids, -1)
        for slot in range(ref.shape[0]):
            found = jnp.where(ref[slot:slot + 1, :] == ids, slot, found)
        out[start:start + span, :] = found
    for start, ref in zip(starts[2:4], (kept_ref, cols_ref)):
        cols = ref[...]
        place = jnp.zeros_like(cols)
        for index, layer in enumerate(layers):
            for row in range(rows):
                place = jnp.where(cols == layer * rows + row, index * rows + row, place)
        out[start:start + ref.shape[0], :] = place


def kernel(count, rows, slots, kept, x_hbm, cols_ref, kept_ref, sq_out, new_out, x_ref, tab, found,
           a, d, sq, new, send_sem, recv_sem, out_sem, in_sem, *bufs):
    width = x_ref.shape[-1]
    part_width = width // HALVES
    load_x = pltpu.make_async_copy(x_hbm, x_ref, in_sem.at[0])
    load_x.start()
    span = LAYERS * rows
    pairs = rows // 2
    me = lax.axis_index("row")
    core, side = me % 2, (me // 2) % 2
    mate = me + 1 - 2 * core
    across = me + 2 - 4 * side
    onward = (me + 4 - 8 * side + count) % count
    behind = (me - 4 + 8 * side + count) % count
    shares_first = core == side
    own, bufs = bufs[:2 * HALVES], bufs[2 * HALVES:]

    barrier = pltpu.get_barrier_semaphore()
    for other in (mate, across, onward, behind):
        pl.semaphore_signal(barrier, inc=1, device_id={"row": other}, device_id_type=MESH)
    pl.semaphore_wait(barrier, 4)

    starts = table_rows(span, slots, kept)
    layers = window_layers(me, count)
    pieces = rows * HALVES

    def landed(source, piece):
        return bufs[(piece // 2) * 4 + source]

    def landing(source, piece):
        return landed(source, piece).at[piece % 2]

    def copy(source, piece, src, device):
        return pltpu.make_async_remote_copy(
            src_ref=src,
            dst_ref=landing(source, piece),
            send_sem=send_sem.at[source, piece],
            recv_sem=recv_sem.at[source, piece],
            device_id={"row": device},
            device_id_type=MESH,
        )

    def own_piece(piece):
        return own[piece // rows].at[piece % rows]

    def to_mate(piece):
        return copy(0, piece, own_piece(piece), mate)

    def to_across(piece):
        return copy(1, piece, own_piece(piece), across)

    def to_onward(piece):
        return copy(2, piece, landing(1, piece), onward)

    def share(piece, source):
        return copy(3, piece, landing(source, piece), mate)

    def block(ref, row, slot):
        value = ref[row, jnp.maximum(slot, 0)]
        return jnp.where(slot >= 0, value, jnp.zeros_like(value))

    def multiply(phase, source, pair):
        stage, half = phase // HALVES, phase % HALVES
        first = source == 0 and pair == 0
        if source == 0:
            ref, base = own[phase], 2 * pair
        else:
            ref, base = bufs[(phase * pairs + pair) * 4 + source - 1], 0
        line = layers[source] * rows + 2 * pair
        group = span // 2

        def body(step, carry):
            left = jnp.concatenate([
                jnp.concatenate(
                    [block(ref, base + row, tab[starts[stage] + group * step + col, line + row])
                     for row in range(2)], axis=1)
                for col in range(group)], axis=0)
            part = jnp.dot(left, a[source * pairs + pair], preferred_element_type=jnp.float32)
            for col in range(group):
                piece = part[col * part_width:(col + 1) * part_width]
                if first:
                    d[half, group * step + col] = piece
                else:
                    d[half, group * step + col] += piece
            return carry

        lax.fori_loop(0, 2, body, 0, unroll=True)

    def near(phase):
        for pair in range(pairs):
            multiply(phase, 0, pair)
        for piece in range(phase * rows, (phase + 1) * rows):
            to_mate(piece).wait_recv()
        for pair in range(pairs):
            multiply(phase, 1, pair)

    def finish(phase):
        stage, half = phase // HALVES, phase % HALVES
        for row in range(rows):
            lanes = pl.ds(row * width, width)
            columns = pl.ds(half * part_width, part_width)
            if stage == 0:
                line = lax.broadcasted_iota(jnp.int32, (part_width, width), 0) + half * part_width
                eye = (line == lax.broadcasted_iota(jnp.int32, (part_width, width), 1)).astype(
                    jnp.float32)

                def pick(slot, carry):
                    place = tab[starts[2] + slot, me * rows + row]
                    value = d[half, place, :, lanes]
                    sq[row, slot, :, columns] = value.T
                    three = jnp.where(place == row, 3.0, 0.0)
                    own[HALVES + half][row, slot] = (three * eye - value).astype(jnp.bfloat16)
                    return carry

                lax.fori_loop(0, kept, pick, 0, unroll=7)
                piece = pieces + half * rows + row
                to_across(piece).start()
                to_mate(piece).start()
                if half == HALVES - 1:
                    pltpu.make_async_copy(sq.at[row], sq_out.at[row], out_sem.at[0, row]).start()
            else:
                def pick(slot, carry):
                    place = tab[starts[3] + slot, me * rows + row]
                    new[row, slot, :, columns] = 0.5 * d[half, place, :, lanes].T
                    return carry

                lax.fori_loop(0, slots, pick, 0, unroll=7)
                if half == HALVES - 1:
                    pltpu.make_async_copy(new.at[row], new_out.at[row], out_sem.at[1, row]).start()

    load_x.wait()
    for half in range(HALVES):
        for row in range(rows):
            def turn(slot, carry):
                own[half][row, slot] = x_ref[row, slot].T[half * part_width:(half + 1) * part_width]
                return carry

            lax.fori_loop(0, slots, turn, 0, unroll=7)
            to_across(half * rows + row).start()
            to_mate(half * rows + row).start()

    fill_tables(cols_ref, kept_ref, found, layers, rows, starts)
    load_tab = pltpu.make_async_copy(found, tab, in_sem.at[1])
    load_tab.start()
    load_tab.wait()

    def build(step, carry):
        for row in range(rows):
            for col in range(2):
                slot = tab[2 * step + col, layers[0] * rows + row]
                for half in range(HALVES):
                    at = col * width + half * part_width
                    a[step, at:at + part_width, row * width:(row + 1) * width] = block(
                        own[half], row, slot)
        return carry

    lax.fori_loop(0, LAYERS * pairs, build, 0)
    near(0)
    near(1)

    lag = 2
    total = 2 * pieces
    for step in range(total + lag):
        if step < total:
            to_across(step).wait_recv()
            to_onward(step).start()

            @pl.when(shares_first)
            def _():
                share(step, 1).start()

        late = step - lag
        if late >= 0:
            to_onward(late).wait_recv()

            @pl.when(jnp.logical_not(shares_first))
            def _():
                share(late, 2).start()

        if step < total and step % 2 == 1:
            multiply(step // rows, 2, step % rows // 2)
        if late >= 0 and late % 2 == 1:
            phase, pair = late // rows, late % rows // 2
            multiply(phase, 3, pair)
            for piece in (late - 1, late):
                share(piece, 1).wait_recv()
            multiply(phase, 4, pair)
            if pair == pairs - 1:
                finish(phase)
                if phase + HALVES < 2 * HALVES:
                    near(phase + HALVES)

    for piece in range(total):
        to_mate(piece).wait_send()
        to_across(piece).wait_send()
        to_onward(piece).wait_send()
        share(piece, 1).wait_send()
    for row in range(rows):
        pltpu.make_async_copy(sq.at[row], sq_out.at[row], out_sem.at[0, row]).wait()
        pltpu.make_async_copy(new.at[row], new_out.at[row], out_sem.at[1, row]).wait()


def local(count, blocks, block_cols, kept_cols):
    rows, slots, width, _ = blocks.shape
    kept = kept_cols.shape[1]
    span = LAYERS * rows
    pieces = rows * HALVES
    half_width = width // HALVES
    own = [
        pltpu.VMEM((rows, depth, half_width, width), jnp.bfloat16)
        for depth in (slots, kept)
        for _ in range(HALVES)
    ]
    landings = [
        pltpu.VMEM((2, depth, half_width, width), jnp.bfloat16)
        for depth in (slots, kept)
        for _ in range(HALVES * 4 * (rows // 2))
    ]
    return pl.pallas_call(
        functools.partial(kernel, count, rows, slots, kept),
        out_shape=(
            jax.ShapeDtypeStruct((rows, kept, width, width), jnp.float32),
            jax.ShapeDtypeStruct((rows, slots, width, width), jnp.float32),
        ),
        in_specs=[pl.BlockSpec(memory_space=pl.ANY)] + [pl.BlockSpec(memory_space=pltpu.VMEM)] * 2,
        out_specs=(pl.BlockSpec(memory_space=pl.ANY), pl.BlockSpec(memory_space=pl.ANY)),
        scratch_shapes=[
            pltpu.VMEM((rows, slots, width, width), jnp.bfloat16),
            pltpu.SMEM((table_rows(span, slots, kept)[-1], block_cols.shape[0]), jnp.int32),
            pltpu.VMEM((table_rows(span, slots, kept)[-1], block_cols.shape[0]), jnp.int32),
            pltpu.VMEM((LAYERS * rows // 2, 2 * width, rows * width), jnp.bfloat16),
            pltpu.VMEM((HALVES, span, half_width, rows * width), jnp.float32),
            pltpu.VMEM((rows, kept, width, width), jnp.float32),
            pltpu.VMEM((rows, slots, width, width), jnp.float32),
            pltpu.SemaphoreType.DMA((4, 2 * pieces)),
            pltpu.SemaphoreType.DMA((4, 2 * pieces)),
            pltpu.SemaphoreType.DMA((2, rows)),
            pltpu.SemaphoreType.DMA((2,)),
        ] + own + landings,
        compiler_params=pltpu.CompilerParams(
            collective_id=0, has_side_effects=True, vmem_limit_bytes=60 * 1024 * 1024
        ),
    )(blocks, block_cols.T, kept_cols.T)


def solution(mesh):
    count = mesh.shape["row"]
    in_specs = (P(("groups", "row"), None, None, None), P("groups", None), P("groups", None))
    out_specs = (P(("groups", "row"), None, None, None), P(("groups", "row"), None, None, None))
    return jax.shard_map(
        functools.partial(local, count), mesh=mesh, in_specs=in_specs, out_specs=out_specs,
        check_vma=False)
```
